32 devices in a mesh: dp: 32 (over z, y, x, core).
Axes of the slice: x: 2, y: 2, z: 4, core: 2. Of those that a mesh axis runs over, the one named last changes fastest.
Arguments:
- tokens: bfloat16 [512, 14, 14, 512], P('dp'), may hold values from -6 to 6
- cotangent: bfloat16 [512, 14, 14, 512], P('dp'), may hold values from -6 to 6
- counts: int32 [32], P('dp'), may hold values from 8 to 16, as said below
- region_ids: int32 [14, 14], replicated, may hold values from 0 to 2
- relative_index: int32 [49, 49], replicated, may hold values from 0 to 168
- attn_gain: bfloat16 [512], P('dp'), may hold values from 0.5 to 1.5
- attn_shift: bfloat16 [512], P('dp'), may hold values from -3 to 3
- qkv_weight: bfloat16 [512, 1536], P('dp'), may hold values from -0.25 to 0.25
- query_bias: bfloat16 [512], P('dp'), may hold values from -3 to 3
- value_bias: bfloat16 [512], P('dp'), may hold values from -3 to 3
- proj_weight: bfloat16 [512, 512], P('dp'), may hold values from -0.75 to 0.75
- proj_bias: bfloat16 [512], P('dp'), may hold values from -3 to 3
- mlp_gain: bfloat16 [512], P('dp'), may hold values from 0.5 to 1.5
- mlp_shift: bfloat16 [512], P('dp'), may hold values from -3 to 3
- hidden_weight: bfloat16 [512, 2048], P('dp'), may hold values from -0.25 to 0.25
- hidden_bias: bfloat16 [2048], P('dp'), may hold values from -3 to 3
- output_weight: bfloat16 [2048, 512], P('dp'), may hold values from -0.125 to 0.125
- output_bias: bfloat16 [512], P('dp'), may hold values from -3 to 3
- bias_table: bfloat16 [169, 16], replicated, may hold values from -4 to 4
Outputs:
- activations: bfloat16 [512, 14, 14, 512], P('dp')
- tokens_grad: bfloat16 [512, 14, 14, 512], P('dp')
- attn_gain_grad: float32 [512], P('dp')
- attn_shift_grad: float32 [512], P('dp')
- qkv_weight_grad: float32 [512, 1536], P('dp')
- query_bias_grad: float32 [512], P('dp')
- value_bias_grad: float32 [512], P('dp')
- proj_weight_grad: float32 [512, 512], P('dp')
- proj_bias_grad: float32 [512], P('dp')
- mlp_gain_grad: float32 [512], P('dp')
- mlp_shift_grad: float32 [512], P('dp')
- hidden_weight_grad: float32 [512, 2048], P('dp')
- hidden_bias_grad: float32 [2048], P('dp')
- output_weight_grad: float32 [2048, 512], P('dp')
- output_bias_grad: float32 [512], P('dp')
- bias_table_grad: float32 [169, 16], replicated
The draws below stay inside these ranges and needn't reach their ends.
Inputs may be any that keep to these rules, and one draw needn't show every extreme that they name: `counts`: each device holds between 8 and 16 images in its first slots; in every draw some device holds 16 and some holds 8.
All inputs are finite; a program needn't handle non-finite values.
Results may differ from the reference program's by a relative error of at most 0.011.
Values may be sent and summed in bfloat16 or wider, within the bound.
A program may use at most 320 MiB of HBM per device.

```python
import jax
import jax.numpy as jnp
from jax import lax

D = 512
HEADS = 16
HEAD = 32
FF = 2048
WIN = 7
MAP = 14
IMG_DEV = 16
SHIFT = 3
TABLE = 169
SLOTS = 512
N_DP = 32


def draw_counts(key, part):
    devices = SLOTS // IMG_DEV
    first_key = jax.random.fold_in(key, 11)
    second_key = jax.random.fold_in(key, 23)
    loads = jax.random.randint(first_key, (devices,), IMG_DEV // 2, IMG_DEV + 1)
    chosen = jax.random.randint(second_key, (), 0, devices)
    places = jnp.arange(devices)
    loads = jnp.where(places == chosen, IMG_DEV, loads)
    loads = jnp.where(places == (chosen + 1) % devices, IMG_DEV // 2, loads)
    return loads.astype(jnp.int32)


def set_ends(drawn, own_key, least, top_value):
    longest = drawn.shape.index(max(drawn.shape))
    spots = []
    for shift in (0, 1):
        where = [jax.random.randint(jax.random.fold_in(own_key, axis), (), 0, length) for axis, length in enumerate(drawn.shape)]
        where[longest] = (where[longest] + shift) % drawn.shape[longest]
        spots.append(tuple(where))
    return drawn.at[spots[0]].set(least).at[spots[1]].set(top_value)


def level_of(own_key, dims, shards, low, high):
    loudness, own = 1.0, jax.random.fold_in(own_key, 6)
    for axis_at, parts in shards:
        draws = jnp.exp(jax.random.uniform(jax.random.fold_in(own, axis_at), (parts,), jnp.float32, low / len(shards), high / len(shards)))
        loudness = loudness * jnp.repeat(draws, dims[axis_at] // parts).reshape([-1 if axis == axis_at else 1 for axis in range(len(dims))])
    return loudness


def normal_values(rng, dims, spread, bound, cuts=(), held_as=jnp.bfloat16):
    drawn = spread * jax.random.normal(rng, dims, jnp.float32)
    if cuts:
        drawn = drawn * level_of(rng, dims, cuts, -0.22, 0.18)
    return jnp.clip(drawn, -bound, bound).astype(held_as)


def setup_inputs(seed: int = 0) -> dict:
    seeds = jax.random.split(jax.random.key(seed), 20)
    tokens = normal_values(seeds[0], (SLOTS, MAP, MAP, D), 1.0, 6.0, ((0, 32),))
    cotangent = normal_values(seeds[1], (SLOTS, MAP, MAP, D), 1.0, 6.0, ((0, 32),))
    counts = draw_counts(jax.random.fold_in(seeds[19], 71), 0)
    region_ids = set_ends(jax.random.randint(seeds[3], (MAP, MAP), 0, 3), jax.random.fold_in(seeds[3], 1), 0, 2).astype(jnp.int32)
    relative_index = set_ends(jax.random.randint(seeds[4], (WIN * WIN, WIN * WIN), 0, TABLE), jax.random.fold_in(seeds[4], 1), 0, TABLE - 1).astype(jnp.int32)
    attn_gain = jnp.clip(1.0 + 0.1 * jax.random.normal(seeds[5], (D,), jnp.float32), 0.5, 1.5).astype(jnp.bfloat16)
    attn_shift = normal_values(seeds[6], (D,), 0.5, 3.0, ((0, 32),))
    qkv_weight = normal_values(seeds[7], (D, 3 * D), D ** -0.5, 0.25, ((0, 32),))
    query_bias = normal_values(seeds[8], (D,), 0.5, 3.0, ((0, 32),))
    value_bias = normal_values(seeds[9], (D,), 0.5, 3.0, ((0, 32),))
    proj_weight = normal_values(seeds[10], (D, D), (D // 8) ** -0.5, 0.75, ((0, 32),))
    proj_bias = normal_values(seeds[11], (D,), 0.5, 3.0, ((0, 32),))
    mlp_gain = jnp.clip(1.0 + 0.1 * jax.random.normal(seeds[12], (D,), jnp.float32), 0.5, 1.5).astype(jnp.bfloat16)
    mlp_shift = normal_values(seeds[13], (D,), 0.5, 3.0, ((0, 32),))
    hidden_weight = normal_values(seeds[14], (D, FF), D ** -0.5, 0.25, ((0, 32),))
    hidden_bias = normal_values(seeds[15], (FF,), 0.5, 3.0, ((0, 32),))
    output_weight = normal_values(seeds[16], (FF, D), FF ** -0.5, 0.125, ((0, 32),))
    output_bias = normal_values(seeds[17], (D,), 0.5, 3.0, ((0, 32),))
    bias_table = normal_values(seeds[18], (TABLE, HEADS), 1.0, 4.0)
    return dict(tokens=tokens, cotangent=cotangent, counts=counts, region_ids=region_ids, relative_index=relative_index, attn_gain=attn_gain, attn_shift=attn_shift, qkv_weight=qkv_weight, query_bias=query_bias, value_bias=value_bias, proj_weight=proj_weight, proj_bias=proj_bias, mlp_gain=mlp_gain, mlp_shift=mlp_shift, hidden_weight=hidden_weight, hidden_bias=hidden_bias, output_weight=output_weight, output_bias=output_bias, bias_table=bias_table)


@jax.custom_vjp
def low(v):
    return lax.optimization_barrier(v.astype(jnp.bfloat16)).astype(jnp.float32)

@jax.custom_vjp
def low_back(v):
    return v

def low_keep(v):
    return (low(v), None)

def low_pass(kept, grad):
    return (grad,)

def back_keep(v):
    return (v, None)

def back_low(kept, grad):
    return (low(grad),)
low.defvjp(low_keep, low_pass)
low_back.defvjp(back_keep, back_low)
EPS = 1e-05
MASK_FILL = -100.0

def highest(left, right):
    return jnp.dot(left, right, precision=lax.Precision.HIGHEST, preferred_element_type=jnp.float32)

def layer_norm(rows, gain, shift):
    mean = lax.optimization_barrier(jnp.mean(rows, axis=-1, keepdims=True))
    centred = rows - mean
    inverse = lax.rsqrt(lax.optimization_barrier(jnp.mean(centred * centred, axis=-1, keepdims=True)) + EPS)
    return centred * inverse * gain + shift

def to_windows(field):
    images = field.shape[0]
    count = MAP // WIN
    rolled = jnp.roll(field, (-SHIFT, -SHIFT), axis=(1, 2))
    blocks = rolled.reshape(images, count, WIN, count, WIN, field.shape[-1])
    return blocks.transpose(0, 1, 3, 2, 4, 5).reshape(images, count * count, WIN * WIN, field.shape[-1])

def from_windows(blocks):
    images = blocks.shape[0]
    count = MAP // WIN
    grid = blocks.reshape(images, count, count, WIN, WIN, blocks.shape[-1])
    grid = grid.transpose(0, 1, 3, 2, 4, 5).reshape(images, MAP, MAP, blocks.shape[-1])
    return jnp.roll(grid, (SHIFT, SHIFT), axis=(1, 2))

def region_mask(region_ids):
    count = MAP // WIN
    cells = region_ids.reshape(count, WIN, count, WIN).transpose(0, 2, 1, 3).reshape(count * count, WIN * WIN)
    same = cells[:, :, None] == cells[:, None, :]
    return jnp.where(same, 0.0, MASK_FILL).astype(jnp.float32)

def forward(params, inputs, valid, mask, relative_index):
    gain_one, shift_one, qkv_full, query_add, value_add, proj_full, proj_add, gain_two, shift_two, hidden_full, hidden_add, out_full, out_add, table = params
    images = inputs.shape[0]
    rows = inputs.reshape(-1, D)
    first_in = low(layer_norm(rows, gain_one, shift_one))
    joined = jnp.concatenate([query_add, jnp.zeros_like(query_add), value_add])
    qkv_rows = low(low_back(highest(first_in, qkv_full) + joined))
    windows = to_windows(qkv_rows.reshape(images, MAP, MAP, 3 * D))
    windows = windows.reshape(images, -1, WIN * WIN, 3, HEADS, HEAD)
    queries, keys, values = (windows[:, :, :, 0], windows[:, :, :, 1], windows[:, :, :, 2])
    position = table[relative_index].transpose(2, 0, 1)
    raw = jnp.einsum('bwqhe,bwkhe->bwhqk', queries, keys, precision=lax.Precision.HIGHEST)
    scores = low_back(raw * HEAD ** (-0.5) + position[None, None] + mask[None, :, None])
    probs = low(jax.nn.softmax(scores, axis=-1))
    mixed = jnp.einsum('bwhqk,bwkhe->bwqhe', probs, values, precision=lax.Precision.HIGHEST)
    mixed = low(low_back(mixed))
    attended = from_windows(mixed.reshape(images, -1, WIN * WIN, D)).reshape(-1, D)
    after_attn = rows + low_back(highest(attended, proj_full) + proj_add)
    second_in = low(layer_norm(after_attn, gain_two, shift_two))
    hidden = low_back(highest(second_in, hidden_full) + hidden_add)
    active = low(jax.nn.gelu(hidden, approximate=False))
    outcome = after_attn + highest(active, out_full) + out_add
    return outcome.reshape(inputs.shape) * valid[:, None, None, None]

def reference(tokens, cotangent, counts, region_ids, relative_index, attn_gain, attn_shift, qkv_weight, query_bias, value_bias, proj_weight, proj_bias, mlp_gain, mlp_shift, hidden_weight, hidden_bias, output_weight, output_bias, bias_table):
    params = tuple((item.astype(jnp.float32) for item in (attn_gain, attn_shift, qkv_weight, query_bias, value_bias, proj_weight, proj_bias, mlp_gain, mlp_shift, hidden_weight, hidden_bias, output_weight, output_bias, bias_table)))
    mask = region_mask(region_ids)
    groups = tokens.astype(jnp.float32).reshape(N_DP, IMG_DEV, MAP, MAP, D)
    cot_groups = cotangent.astype(jnp.float32).reshape(N_DP, IMG_DEV, MAP, MAP, D)

    def one_group(carry, item):
        inputs, cot_group, count = item
        valid = (jnp.arange(IMG_DEV) < count).astype(jnp.float32)

        def run(weights, values):
            return forward(weights, values, valid, mask, relative_index)
        outcome, pull = jax.vjp(run, params, inputs)
        grad_params, grad_inputs = pull(cot_group)
        carry = jax.tree.map(lambda left, right: left + right, carry, grad_params)
        return (carry, (outcome.astype(jnp.bfloat16), grad_inputs.astype(jnp.bfloat16)))
    zeros = tuple((jnp.zeros_like(item) for item in params))
    grads, (outcomes, grad_tokens) = lax.scan(one_group, zeros, (groups, cot_groups, counts))
    activations = outcomes.reshape(tokens.shape)
    tokens_grad = grad_tokens.reshape(tokens.shape)
    return (activations, tokens_grad, grads[0], grads[1], grads[2], grads[3], grads[4], grads[5], grads[6], grads[7], grads[8], grads[9], grads[10], grads[11], grads[12], grads[13])
```

```python
import functools
import math

import jax
import jax.numpy as jnp
from jax import lax
from jax.experimental import pallas as pl
from jax.experimental.pallas import tpu as pltpu
from jax.sharding import PartitionSpec as P

WIN = 7
MAP = 14
SHIFT = 3
SPAN = WIN * WIN
PAD = 64
GROUP = 2
EPS = 1e-05
MASK_FILL = -100.0
NEG = -1e30
F32 = jnp.float32
BF16 = jnp.bfloat16


def to_windows(field):
    images = field.shape[0]
    count = MAP // WIN
    rolled = jnp.roll(field, (-SHIFT, -SHIFT), axis=(1, 2))
    blocks = rolled.reshape(images, count, WIN, count, WIN, field.shape[-1])
    blocks = blocks.transpose(0, 1, 3, 2, 4, 5).reshape(
        images, count * count, SPAN, field.shape[-1]
    )
    blocks = jnp.pad(blocks, ((0, 0), (0, 0), (0, PAD - SPAN), (0, 0)))
    return blocks.reshape(images, count * count * PAD, field.shape[-1])


def from_windows(blocks):
    images = blocks.shape[0]
    count = MAP // WIN
    blocks = blocks.reshape(images, count * count, PAD, blocks.shape[-1])[:, :, :SPAN]
    grid = blocks.reshape(images, count, count, WIN, WIN, blocks.shape[-1])
    grid = grid.transpose(0, 1, 3, 2, 4, 5).reshape(images, MAP, MAP, blocks.shape[-1])
    return jnp.roll(grid, (SHIFT, SHIFT), axis=(1, 2))


def nn(a, b):
    return jnp.dot(a, b, preferred_element_type=F32)


def nt(a, b):
    return lax.dot_general(a, b, (((1,), (1,)), ((), ())), preferred_element_type=F32)


def tn(a, b):
    return lax.dot_general(a, b, (((0,), (0,)), ((), ())), preferred_element_type=F32)


def row_mean(values):
    return jnp.mean(values, axis=-1, keepdims=True)


def block_kernel(
    counts,
    x_ref,
    c_ref,
    w_ref,
    v_ref,
    bias_ref,
    act_ref,
    tg_ref,
    gw_ref,
    gv_ref,
    gs_ref,
    acc,
    p_s,
    qkv_s,
    mixed_s,
    gm_s,
    gqkv_s,
    first_s,
    n1_s,
    *,
    scale,
):
    step = pl.program_id(0)
    rows = x_ref.shape[0] * x_ref.shape[1]
    per_image = x_ref.shape[1]
    width = x_ref.shape[2]
    lane = lax.broadcasted_iota(jnp.int32, (1, 128), 1) // 32
    lane_masks = [lane == h for h in range(4)]
    zero_low = jnp.zeros((), BF16)

    @pl.when(step == 0)
    def _():
        acc[...] = jnp.zeros_like(acc)
        gv_ref[...] = jnp.zeros_like(gv_ref)
        gs_ref[...] = jnp.zeros_like(gs_ref)

    def vec(i):
        return v_ref[i : i + 1, :]

    def stacked(a):
        return jnp.concatenate([jnp.where(m, a, zero_low) for m in lane_masks], axis=0)

    def unstacked(a):
        total = jnp.where(lane_masks[0], a[0:128], 0.0)
        for h in range(1, 4):
            total = jnp.where(lane_masks[h], a[128 * h : 128 * (h + 1)], total)
        return total

    ones = jnp.ones((8, rows), BF16)

    def add_vec(i, total):
        gv_ref[i : i + 1, :] += total

    def low_total(a):
        return nn(ones, a)[0:1]

    x = x_ref[...].reshape(rows, width).astype(F32)
    centred = x - row_mean(x)
    r1 = lax.rsqrt(row_mean(centred * centred) + EPS)
    n1 = centred * r1
    n1_s[...] = n1
    first = (n1 * vec(0) + vec(1)).astype(BF16)
    first_s[...] = first
    qkv_s[:, 0:width] = (nn(first, w_ref[0]) + vec(2)).astype(BF16)
    qkv_s[:, width : 2 * width] = nn(first, w_ref[1]).astype(BF16)
    qkv_s[:, 2 * width : 3 * width] = (nn(first, w_ref[2]) + vec(3)).astype(BF16)

    def forward_pair(pr, carry):
        at = pl.ds(pl.multiple_of(pr * 128, 128), 128)
        pair = lax.rem(pr, 2)
        for g in range(4):
            q = qkv_s[at, 128 * g : 128 * (g + 1)]
            k = qkv_s[at, width + 128 * g : width + 128 * (g + 1)]
            v = qkv_s[at, 2 * width + 128 * g : 2 * width + 128 * (g + 1)]
            s = nt(stacked(k), q) * scale + bias_ref[pair, g]
            s = s.reshape(4, 128, 128)
            e = jnp.exp(s - jnp.max(s, axis=1, keepdims=True))
            p = e * (1.0 / jnp.sum(e, axis=1, keepdims=True))
            p = p.reshape(512, 128)
            p_s[pr, g] = p
            mixed_s[at, 128 * g : 128 * (g + 1)] = tn(p.astype(BF16), stacked(v)).astype(BF16)
        return carry

    lax.fori_loop(0, rows // 128, forward_pair, 0)

    after = x + nn(mixed_s[...], w_ref[3]) + vec(4)
    centred = after - row_mean(after)
    r2 = lax.rsqrt(row_mean(centred * centred) + EPS)
    n2 = centred * r2
    second = (n2 * vec(5) + vec(6)).astype(BF16)
    image = step * GROUP + lax.broadcasted_iota(jnp.int32, (rows, 1), 0) // per_image
    valid = image < counts[0]
    go = jnp.where(valid, c_ref[...].reshape(rows, width).astype(F32), 0.0)
    gob = go.astype(BF16)
    add_vec(7, low_total(gob))
    outcome = after + vec(7)
    e2 = None
    for j in range(4):
        hidden = nn(second, w_ref[4 + j]) + vec(8 + j)
        cumulative = 0.5 * (1.0 + lax.erf(hidden * (1.0 / math.sqrt(2.0))))
        density = jnp.exp(-0.5 * hidden * hidden) * (1.0 / math.sqrt(2.0 * math.pi))
        active = (hidden * cumulative).astype(BF16)
        slope = cumulative + hidden * density
        outcome = outcome + nn(active, w_ref[8 + j])
        gh = (nt(gob, w_ref[8 + j]) * slope).astype(BF16)
        acc[8 + j] += tn(active, gob)
        acc[4 + j] += tn(second, gh)
        add_vec(8 + j, low_total(gh))
        part = nt(gh, w_ref[4 + j])
        e2 = part if e2 is None else e2 + part
    act_ref[...] = jnp.where(valid, outcome, 0.0).astype(BF16).reshape(act_ref.shape)
    add_vec(5, jnp.sum(e2 * n2, axis=0, keepdims=True))
    add_vec(6, jnp.sum(e2, axis=0, keepdims=True))
    f = e2 * vec(5)
    grad_after = go + r2 * (f - row_mean(f) - n2 * row_mean(f * n2))
    gp = grad_after.astype(BF16)
    acc[3] += tn(mixed_s[...], gp)
    add_vec(4, low_total(gp))
    gm_s[...] = nt(gp, w_ref[3]).astype(BF16)

    def backward_pair(pr, carry):
        at = pl.ds(pl.multiple_of(pr * 128, 128), 128)
        for g in range(4):
            q = qkv_s[at, 128 * g : 128 * (g + 1)]
            k = qkv_s[at, width + 128 * g : width + 128 * (g + 1)]
            v = qkv_s[at, 2 * width + 128 * g : 2 * width + 128 * (g + 1)]
            gm = gm_s[at, 128 * g : 128 * (g + 1)]
            p = p_s[pr, g]
            dp = nt(stacked(v), gm)
            dv = unstacked(nn(p.astype(BF16), gm))
            inner = jnp.sum((p * dp).reshape(4, 128, 128), axis=1, keepdims=True)
            ds = (p.reshape(4, 128, 128) * (dp.reshape(4, 128, 128) - inner)).reshape(512, 128)
            dsb = ds.astype(BF16)
            gs_ref[g] += dsb.astype(F32)
            dk = unstacked(nn(dsb, q)) * scale
            dq = tn(dsb, stacked(k)) * scale
            gqkv_s[at, 128 * g : 128 * (g + 1)] = dq.astype(BF16)
            gqkv_s[at, width + 128 * g : width + 128 * (g + 1)] = dk.astype(BF16)
            gqkv_s[at, 2 * width + 128 * g : 2 * width + 128 * (g + 1)] = dv.astype(BF16)
        return carry

    lax.fori_loop(0, rows // 128, backward_pair, 0)

    first = first_s[...]
    e1 = None
    for j in range(3):
        gq = gqkv_s[:, width * j : width * (j + 1)]
        acc[j] += tn(first, gq)
        part = nt(gq, w_ref[j])
        e1 = part if e1 is None else e1 + part
        if j == 0:
            add_vec(2, low_total(gq))
        if j == 2:
            add_vec(3, low_total(gq))
    n1 = n1_s[...]
    add_vec(0, jnp.sum(e1 * n1, axis=0, keepdims=True))
    add_vec(1, jnp.sum(e1, axis=0, keepdims=True))
    f = e1 * vec(0)
    grad_in = grad_after + r1 * (f - row_mean(f) - n1 * row_mean(f * n1))
    tg_ref[...] = grad_in.astype(BF16).reshape(tg_ref.shape)

    @pl.when(step == pl.num_programs(0) - 1)
    def _():
        for j in range(12):
            gw_ref[j] = acc[j].astype(BF16)


def run_block(counts, x, c, weights, vectors, bias, scale):
    images, per_image, width = x.shape
    rows = GROUP * per_image
    whole = functools.partial(pl.BlockSpec, pipeline_mode=pl.Buffered(1))
    tile = pl.BlockSpec((GROUP, per_image, width), lambda i: (i, 0, 0))
    return pl.pallas_call(
        functools.partial(block_kernel, scale=scale),
        grid=(images // GROUP,),
        in_specs=[
            pl.BlockSpec(memory_space=pltpu.SMEM),
            tile,
            tile,
            whole(weights.shape, lambda i: (0, 0, 0)),
            whole(vectors.shape, lambda i: (0, 0)),
            whole(bias.shape, lambda i: (0, 0, 0, 0)),
        ],
        out_specs=[
            tile,
            tile,
            whole(weights.shape, lambda i: (0, 0, 0)),
            pl.BlockSpec(vectors.shape, lambda i: (0, 0)),
            pl.BlockSpec((4, 512, 128), lambda i: (0, 0, 0)),
        ],
        out_shape=[
            jax.ShapeDtypeStruct(x.shape, BF16),
            jax.ShapeDtypeStruct(x.shape, BF16),
            jax.ShapeDtypeStruct(weights.shape, BF16),
            jax.ShapeDtypeStruct(vectors.shape, F32),
            jax.ShapeDtypeStruct((4, 512, 128), F32),
        ],
        scratch_shapes=[
            pltpu.VMEM(weights.shape, F32),
            pltpu.VMEM((rows // 128, 4, 512, 128), F32),
            pltpu.VMEM((rows, 3 * width), BF16),
            pltpu.VMEM((rows, width), BF16),
            pltpu.VMEM((rows, width), BF16),
            pltpu.VMEM((rows, 3 * width), BF16),
            pltpu.VMEM((rows, width), BF16),
            pltpu.VMEM((rows, width), F32),
        ],
        compiler_params=pltpu.CompilerParams(
            dimension_semantics=("arbitrary",), vmem_limit_bytes=60 * 1024 * 1024
        ),
    )(counts, x, c, weights, vectors, bias)


def bit_orders(count):
    bits = count.bit_length() - 1
    far = list(range(bits - 1, 0, -1))
    orders = []
    for turn in range(3):
        cut = (turn * len(far)) // 3
        orders.append(far[cut:] + far[:cut] + [0])
    return orders


def swap(array, bit, count):
    return lax.ppermute(array, "dp", [(i, i ^ (1 << bit)) for i in range(count)])


def gather_all(block, order, count, me):
    buffer = block
    for level, bit in enumerate(order):
        other = swap(buffer, bit, count)
        high = ((me >> bit) & 1) == 1
        buffer = jnp.stack(
            [jnp.where(high, other, buffer), jnp.where(high, buffer, other)], axis=level
        )
    bits = len(order)
    back = [order.index(b) for b in range(bits - 1, -1, -1)]
    buffer = buffer.transpose(*back, *range(bits, bits + block.ndim))
    return buffer.reshape(count, *block.shape)


def scatter_sum(blocks, order, count, me):
    bits = len(order)
    buffer = blocks.reshape(*([2] * bits), *blocks.shape[1:])
    left = list(range(bits - 1, -1, -1))
    for bit in order:
        axis = left.index(bit)
        mine = (me >> bit) & 1
        keep = lax.dynamic_index_in_dim(buffer, mine, axis, keepdims=False)
        send = lax.dynamic_index_in_dim(buffer, 1 - mine, axis, keepdims=False)
        got = swap(send, bit, count)
        buffer = (keep.astype(F32) + got.astype(F32)).astype(BF16)
        left.remove(bit)
    return buffer


def local(
    tokens,
    cotangent,
    counts,
    region_ids,
    relative_index,
    attn_gain,
    attn_shift,
    qkv_weight,
    query_bias,
    value_bias,
    proj_weight,
    proj_bias,
    mlp_gain,
    mlp_shift,
    hidden_weight,
    hidden_bias,
    output_weight,
    output_bias,
    bias_table,
    *,
    count,
):
    me = lax.axis_index("dp")
    width = tokens.shape[-1]
    heads = bias_table.shape[1]
    table_rows = bias_table.shape[0]
    scale = (width // heads) ** (-0.5)
    share = qkv_weight.shape[0]
    wide = hidden_bias.shape[0]
    orders = bit_orders(count)

    small = jnp.concatenate(
        [
            attn_gain,
            attn_shift,
            query_bias,
            value_bias,
            proj_bias,
            mlp_gain,
            mlp_shift,
            output_bias,
            hidden_bias,
        ]
    )
    small_len = small.shape[0]
    small = jnp.pad(small, (0, width - small_len)).reshape(1, width)
    pack_one = jnp.concatenate(
        [qkv_weight[:, width * j : width * (j + 1)] for j in range(3)] + [proj_weight], axis=0
    )
    pack_two = jnp.concatenate(
        [hidden_weight[:, width * j : width * (j + 1)] for j in range(4)] + [small], axis=0
    )
    got_one = gather_all(pack_one, orders[0], count, me)
    got_two = gather_all(pack_two, orders[1], count, me)
    got_three = gather_all(output_weight, orders[2], count, me)

    def joined(got):
        return got[:, : 4 * share].reshape(count, 4, share, width).transpose(1, 0, 2, 3).reshape(
            4, width, width
        )

    weights = jnp.concatenate(
        [joined(got_one), joined(got_two), got_three.reshape(4, width, width)], axis=0
    )
    got_small = got_two[:, 4 * share, :small_len].astype(F32)
    vectors = jnp.concatenate(
        [
            got_small[:, : 8 * share].reshape(count, 8, share).transpose(1, 0, 2).reshape(8, width),
            got_small[:, 8 * share :].reshape(4, width),
            jnp.zeros((4, width), F32),
        ],
        axis=0,
    )

    n_win = (MAP // WIN) ** 2
    cells = (
        region_ids.reshape(MAP // WIN, WIN, MAP // WIN, WIN)
        .transpose(0, 2, 1, 3)
        .reshape(n_win, SPAN)
    )
    mask = jnp.where(cells[:, :, None] == cells[:, None, :], 0.0, MASK_FILL).astype(F32)
    mask = jnp.pad(mask, ((0, 0), (0, 0), (0, PAD - SPAN)))
    mask = jnp.pad(mask, ((0, 0), (0, PAD - SPAN), (0, 0)), constant_values=NEG)
    by_key = relative_index.T
    padded_index = jnp.pad(by_key, ((0, PAD - SPAN), (0, PAD - SPAN)), constant_values=-1)
    hot = (jnp.arange(table_rows)[:, None] == padded_index.reshape(1, -1)).astype(BF16)
    position = tn(bias_table, hot).reshape(heads, PAD, PAD)
    per_window = position[None] + mask[:, None]
    per_pair = per_window.reshape(n_win // 2, 2, heads, PAD, PAD)
    off = jnp.full((n_win // 2, heads, PAD, PAD), NEG, F32)
    bias = jnp.concatenate(
        [
            jnp.concatenate([per_pair[:, 0], off], axis=-1),
            jnp.concatenate([off, per_pair[:, 1]], axis=-1),
        ],
        axis=-2,
    ).reshape(n_win // 2, 4, 512, 128)

    act, tg, gw, gv, gs = run_block(
        counts, to_windows(tokens), to_windows(cotangent), weights, vectors, bias, scale
    )

    def cut(four):
        return four.reshape(4, count, share, width).transpose(1, 0, 2, 3).reshape(
            count, 4 * share, width
        )

    small_grad = jnp.concatenate(
        [
            gv[:8].reshape(8, count, share).transpose(1, 0, 2).reshape(count, 8 * share),
            gv[8:12].reshape(count, wide),
        ],
        axis=1,
    ).astype(BF16)
    small_grad = jnp.pad(small_grad, ((0, 0), (0, width - small_len)))[:, None]
    own_one = scatter_sum(cut(gw[0:4]), orders[0][::-1], count, me).astype(F32)
    own_two = scatter_sum(
        jnp.concatenate([cut(gw[4:8]), small_grad], axis=1), orders[1][::-1], count, me
    ).astype(F32)
    own_three = scatter_sum(
        gw[8:12].reshape(count, 4 * share, width), orders[2][::-1], count, me
    ).astype(F32)

    gs = gs.reshape(heads, 128, 128)
    gs = gs[:, :SPAN, :SPAN] + gs[:, PAD : PAD + SPAN, PAD : PAD + SPAN]
    hot_back = (by_key.reshape(-1, 1) == jnp.arange(table_rows)[None, :]).astype(F32)
    table = jnp.dot(
        gs.reshape(heads, SPAN * SPAN),
        hot_back,
        precision=lax.Precision.HIGHEST,
        preferred_element_type=F32,
    )
    for bit in orders[0][::-1]:
        table = table + swap(table, bit, count)

    own_small = own_two[4 * share]

    def piece(i):
        return own_small[i * share : (i + 1) * share]

    return (
        from_windows(act),
        from_windows(tg),
        piece(0),
        piece(1),
        jnp.concatenate([own_one[share * j : share * (j + 1)] for j in range(3)], axis=1),
        piece(2),
        piece(3),
        own_one[3 * share :],
        piece(4),
        piece(5),
        piece(6),
        jnp.concatenate([own_two[share * j : share * (j + 1)] for j in range(4)], axis=1),
        own_small[8 * share : 8 * share + wide],
        own_three,
        piece(7),
        table.T,
    )


def solution(mesh):
    row = P("dp")
    matrix = P("dp", None)
    field = P("dp", None, None, None)
    return jax.shard_map(
        functools.partial(local, count=mesh.shape["dp"]),
        mesh=mesh,
        in_specs=(
            field,
            field,
            row,
            P(),
            P(),
            row,
            row,
            matrix,
            row,
            row,
            matrix,
            row,
            row,
            row,
            matrix,
            row,
            matrix,
            row,
            P(),
        ),
        out_specs=(
            field,
            field,
            row,
            row,
            matrix,
            row,
            row,
            matrix,
            row,
            row,
            row,
            matrix,
            row,
            matrix,
            row,
            P(),
        ),
        check_vma=False,
    )
```

```python
import functools
import math

import jax
import jax.numpy as jnp
from jax import lax
from jax.experimental import pallas as pl
from jax.experimental.pallas import tpu as pltpu
from jax.sharding import PartitionSpec as P

WIN = 7
MAP = 14
SHIFT = 3
SPAN = WIN * WIN
PAD = 64
GROUP = 2
EPS = 1e-05
MASK_FILL = -100.0
NEG = -1e30
F32 = jnp.float32
BF16 = jnp.bfloat16


def to_windows(field):
    images = field.shape[0]
    count = MAP // WIN
    rolled = jnp.roll(field, (-SHIFT, -SHIFT), axis=(1, 2))
    blocks = rolled.reshape(images, count, WIN, count, WIN, field.shape[-1])
    blocks = blocks.transpose(0, 1, 3, 2, 4, 5).reshape(
        images, count * count, SPAN, field.shape[-1]
    )
    blocks = jnp.pad(blocks, ((0, 0), (0, 0), (0, PAD - SPAN), (0, 0)))
    return blocks.reshape(images, count * count * PAD, field.shape[-1])


def from_windows(blocks):
    images = blocks.shape[0]
    count = MAP // WIN
    blocks = blocks.reshape(images, count * count, PAD, blocks.shape[-1])[:, :, :SPAN]
    grid = blocks.reshape(images, count, count, WIN, WIN, blocks.shape[-1])
    grid = grid.transpose(0, 1, 3, 2, 4, 5).reshape(images, MAP, MAP, blocks.shape[-1])
    return jnp.roll(grid, (SHIFT, SHIFT), axis=(1, 2))


def nn(a, b):
    return jnp.dot(a, b, preferred_element_type=F32)


def nt(a, b):
    return lax.dot_general(a, b, (((1,), (1,)), ((), ())), preferred_element_type=F32)


def tn(a, b):
    return lax.dot_general(a, b, (((0,), (0,)), ((), ())), preferred_element_type=F32)


def row_mean(values):
    return jnp.mean(values, axis=-1, keepdims=True)


def block_kernel(
    counts,
    x_ref,
    c_ref,
    a_ref,
    h_ref,
    o_ref,
    v_ref,
    bias_ref,
    act_ref,
    tg_ref,
    ga_ref,
    gh_ref,
    go_ref,
    gv_ref,
    gs_ref,
    acc,
    p_s,
    qkv_s,
    mixed_s,
    gm_s,
    gqkv_s,
    first_s,
    n1_s,
    *,
    scale,
):
    step = pl.program_id(0)
    rows = x_ref.shape[0] * x_ref.shape[1]
    per_image = x_ref.shape[1]
    width = x_ref.shape[2]
    lane = lax.broadcasted_iota(jnp.int32, (1, 128), 1) // 32
    lane_masks = [lane == h for h in range(4)]
    zero_low = jnp.zeros((), BF16)

    @pl.when(step == 0)
    def _():
        acc[...] = jnp.zeros_like(acc)
        gv_ref[...] = jnp.zeros_like(gv_ref)
        gs_ref[...] = jnp.zeros_like(gs_ref)

    def vec(i):
        return v_ref[i : i + 1, :]

    def stacked(a):
        return jnp.concatenate([jnp.where(m, a, zero_low) for m in lane_masks], axis=0)

    def unstacked(a):
        total = jnp.where(lane_masks[0], a[0:128], 0.0)
        for h in range(1, 4):
            total = jnp.where(lane_masks[h], a[128 * h : 128 * (h + 1)], total)
        return total

    ones = jnp.ones((8, rows), BF16)

    def add_vec(i, total):
        gv_ref[i : i + 1, :] += total

    def low_total(a):
        return nn(ones, a)[0:1]

    x = x_ref[...].reshape(rows, width).astype(F32)
    centred = x - row_mean(x)
    r1 = lax.rsqrt(row_mean(centred * centred) + EPS)
    n1 = centred * r1
    n1_s[...] = n1
    first = (n1 * vec(0) + vec(1)).astype(BF16)
    first_s[...] = first
    qkv_s[:, 0:width] = (nn(first, a_ref[0]) + vec(2)).astype(BF16)
    qkv_s[:, width : 2 * width] = nn(first, a_ref[1]).astype(BF16)
    qkv_s[:, 2 * width : 3 * width] = (nn(first, a_ref[2]) + vec(3)).astype(BF16)

    def forward_pair(pr, carry):
        at = pl.ds(pl.multiple_of(pr * 128, 128), 128)
        pair = lax.rem(pr, 2)
        for g in range(4):
            q = qkv_s[at, 128 * g : 128 * (g + 1)]
            k = qkv_s[at, width + 128 * g : width + 128 * (g + 1)]
            v = qkv_s[at, 2 * width + 128 * g : 2 * width + 128 * (g + 1)]
            s = nt(stacked(k), q) * scale + bias_ref[pair, g]
            s = s.reshape(4, 128, 128)
            e = jnp.exp(s - jnp.max(s, axis=1, keepdims=True))
            p = e * (1.0 / jnp.sum(e, axis=1, keepdims=True))
            p = p.reshape(512, 128)
            p_s[pr, g] = p
            mixed_s[at, 128 * g : 128 * (g + 1)] = tn(p.astype(BF16), stacked(v)).astype(BF16)
        return carry

    lax.fori_loop(0, rows // 128, forward_pair, 0)

    after = x + nn(mixed_s[...], a_ref[3]) + vec(4)
    centred = after - row_mean(after)
    r2 = lax.rsqrt(row_mean(centred * centred) + EPS)
    n2 = centred * r2
    second = (n2 * vec(5) + vec(6)).astype(BF16)
    image = step * GROUP + lax.broadcasted_iota(jnp.int32, (rows, 1), 0) // per_image
    valid = image < counts[0]
    go = jnp.where(valid, c_ref[...].reshape(rows, width).astype(F32), 0.0)
    gob = go.astype(BF16)
    add_vec(7, low_total(gob))
    outcome = after + vec(7)
    e2 = None
    for j in range(4):
        hidden = nn(second, h_ref[j]) + vec(8 + j)
        cumulative = 0.5 * (1.0 + lax.erf(hidden * (1.0 / math.sqrt(2.0))))
        density = jnp.exp(-0.5 * hidden * hidden) * (1.0 / math.sqrt(2.0 * math.pi))
        active = (hidden * cumulative).astype(BF16)
        slope = cumulative + hidden * density
        outcome = outcome + nn(active, o_ref[j])
        gh = (nt(gob, o_ref[j]) * slope).astype(BF16)
        acc[8 + j] += tn(active, gob)
        acc[4 + j] += tn(second, gh)
        add_vec(8 + j, low_total(gh))
        part = nt(gh, h_ref[j])
        e2 = part if e2 is None else e2 + part
    act_ref[...] = jnp.where(valid, outcome, 0.0).astype(BF16).reshape(act_ref.shape)
    add_vec(5, jnp.sum(e2 * n2, axis=0, keepdims=True))
    add_vec(6, jnp.sum(e2, axis=0, keepdims=True))
    f = e2 * vec(5)
    grad_after = go + r2 * (f - row_mean(f) - n2 * row_mean(f * n2))
    gp = grad_after.astype(BF16)
    acc[3] += tn(mixed_s[...], gp)
    add_vec(4, low_total(gp))
    gm_s[...] = nt(gp, a_ref[3]).astype(BF16)

    def backward_pair(pr, carry):
        at = pl.ds(pl.multiple_of(pr * 128, 128), 128)
        for g in range(4):
            q = qkv_s[at, 128 * g : 128 * (g + 1)]
            k = qkv_s[at, width + 128 * g : width + 128 * (g + 1)]
            v = qkv_s[at, 2 * width + 128 * g : 2 * width + 128 * (g + 1)]
            gm = gm_s[at, 128 * g : 128 * (g + 1)]
            p = p_s[pr, g]
            dp = nt(stacked(v), gm)
            dv = unstacked(nn(p.astype(BF16), gm))
            inner = jnp.sum((p * dp).reshape(4, 128, 128), axis=1, keepdims=True)
            ds = (p.reshape(4, 128, 128) * (dp.reshape(4, 128, 128) - inner)).reshape(512, 128)
            dsb = ds.astype(BF16)
            gs_ref[g] += dsb.astype(F32)
            dk = unstacked(nn(dsb, q)) * scale
            dq = tn(dsb, stacked(k)) * scale
            gqkv_s[at, 128 * g : 128 * (g + 1)] = dq.astype(BF16)
            gqkv_s[at, width + 128 * g : width + 128 * (g + 1)] = dk.astype(BF16)
            gqkv_s[at, 2 * width + 128 * g : 2 * width + 128 * (g + 1)] = dv.astype(BF16)
        return carry

    lax.fori_loop(0, rows // 128, backward_pair, 0)

    first = first_s[...]
    e1 = None
    for j in range(3):
        gq = gqkv_s[:, width * j : width * (j + 1)]
        acc[j] += tn(first, gq)
        part = nt(gq, a_ref[j])
        e1 = part if e1 is None else e1 + part
        if j == 0:
            add_vec(2, low_total(gq))
        if j == 2:
            add_vec(3, low_total(gq))
    n1 = n1_s[...]
    add_vec(0, jnp.sum(e1 * n1, axis=0, keepdims=True))
    add_vec(1, jnp.sum(e1, axis=0, keepdims=True))
    f = e1 * vec(0)
    grad_in = grad_after + r1 * (f - row_mean(f) - n1 * row_mean(f * n1))
    tg_ref[...] = grad_in.astype(BF16).reshape(tg_ref.shape)

    @pl.when(step == pl.num_programs(0) - 1)
    def _():
        for j in range(4):
            ga_ref[j] = acc[j].astype(BF16)
            gh_ref[j] = acc[4 + j].astype(BF16)
            go_ref[j] = acc[8 + j].astype(BF16)


def run_block(counts, x, c, parts, vectors, bias, scale):
    images, per_image, width = x.shape
    rows = GROUP * per_image
    whole = functools.partial(pl.BlockSpec, pipeline_mode=pl.Buffered(1))
    tile = pl.BlockSpec((GROUP, per_image, width), lambda i: (i, 0, 0))
    return pl.pallas_call(
        functools.partial(block_kernel, scale=scale),
        grid=(images // GROUP,),
        in_specs=[
            pl.BlockSpec(memory_space=pltpu.SMEM),
            tile,
            tile,
            *[whole(part.shape, lambda i: (0, 0, 0)) for part in parts],
            whole(vectors.shape, lambda i: (0, 0)),
            whole(bias.shape, lambda i: (0, 0, 0, 0)),
        ],
        out_specs=[
            tile,
            tile,
            *[whole(part.shape, lambda i: (0, 0, 0)) for part in parts],
            pl.BlockSpec(vectors.shape, lambda i: (0, 0)),
            pl.BlockSpec((4, 512, 128), lambda i: (0, 0, 0)),
        ],
        out_shape=[
            jax.ShapeDtypeStruct(x.shape, BF16),
            jax.ShapeDtypeStruct(x.shape, BF16),
            *[jax.ShapeDtypeStruct(part.shape, BF16) for part in parts],
            jax.ShapeDtypeStruct(vectors.shape, F32),
            jax.ShapeDtypeStruct((4, 512, 128), F32),
        ],
        scratch_shapes=[
            pltpu.VMEM((3 * parts[0].shape[0], *parts[0].shape[1:]), F32),
            pltpu.VMEM((rows // 128, 4, 512, 128), F32),
            pltpu.VMEM((rows, 3 * width), BF16),
            pltpu.VMEM((rows, width), BF16),
            pltpu.VMEM((rows, width), BF16),
            pltpu.VMEM((rows, 3 * width), BF16),
            pltpu.VMEM((rows, width), BF16),
            pltpu.VMEM((rows, width), F32),
        ],
        compiler_params=pltpu.CompilerParams(
            dimension_semantics=("arbitrary",), vmem_limit_bytes=60 * 1024 * 1024
        ),
    )(counts, x, c, *parts, vectors, bias)


def bit_orders(count):
    bits = count.bit_length() - 1
    far = list(range(bits - 1, 0, -1))
    orders = []
    for turn in range(3):
        rest = far[1:]
        cut = (turn * len(rest)) // 3
        orders.append(far[:1] + rest[cut:] + rest[:cut] + [0])
    return orders


def swap(array, bit, count):
    return lax.ppermute(array, "dp", [(i, i ^ (1 << bit)) for i in range(count)])


def gather_all(block, order, count, me, beside=None):
    buffer = block
    for level, bit in enumerate(order):
        if beside is not None and level == len(order) - 1:
            buffer, beside = lax.optimization_barrier((buffer, beside))
        other = swap(buffer, bit, count)
        high = ((me >> bit) & 1) == 1
        buffer = jnp.stack(
            [jnp.where(high, other, buffer), jnp.where(high, buffer, other)], axis=level
        )
    bits = len(order)
    back = [order.index(b) for b in range(bits - 1, -1, -1)]
    buffer = buffer.transpose(*back, *range(bits, bits + block.ndim))
    return buffer.reshape(count, *block.shape), beside


def scatter_sum(blocks, order, count, me):
    bits = len(order)
    buffer = blocks.reshape(*([2] * bits), *blocks.shape[1:])
    left = list(range(bits - 1, -1, -1))
    for bit in order:
        axis = left.index(bit)
        mine = (me >> bit) & 1
        keep = lax.dynamic_index_in_dim(buffer, mine, axis, keepdims=False)
        send = lax.dynamic_index_in_dim(buffer, 1 - mine, axis, keepdims=False)
        got = swap(send, bit, count)
        buffer = (keep.astype(F32) + got.astype(F32)).astype(BF16)
        left.remove(bit)
    return buffer


def local(
    tokens,
    cotangent,
    counts,
    region_ids,
    relative_index,
    attn_gain,
    attn_shift,
    qkv_weight,
    query_bias,
    value_bias,
    proj_weight,
    proj_bias,
    mlp_gain,
    mlp_shift,
    hidden_weight,
    hidden_bias,
    output_weight,
    output_bias,
    bias_table,
    *,
    count,
):
    me = lax.axis_index("dp")
    width = tokens.shape[-1]
    heads = bias_table.shape[1]
    table_rows = bias_table.shape[0]
    scale = (width // heads) ** (-0.5)
    share = qkv_weight.shape[0]
    wide = hidden_bias.shape[0]
    orders = bit_orders(count)

    small = jnp.concatenate(
        [
            attn_gain,
            attn_shift,
            query_bias,
            value_bias,
            proj_bias,
            mlp_gain,
            mlp_shift,
            output_bias,
            hidden_bias,
        ]
    )
    small_len = small.shape[0]
    small = jnp.pad(small, (0, width - small_len)).reshape(1, width)
    pack_one = jnp.concatenate(
        [qkv_weight[:, width * j : width * (j + 1)] for j in range(3)] + [proj_weight], axis=0
    )
    pack_two = jnp.concatenate(
        [hidden_weight[:, width * j : width * (j + 1)] for j in range(4)], axis=0
    )
    got_small, _ = gather_all(small, orders[0], count, me)
    got_one, x_rows = gather_all(pack_one, orders[0], count, me, to_windows(tokens))
    got_two, c_rows = gather_all(pack_two, orders[1], count, me, to_windows(cotangent))
    got_three, _ = gather_all(output_weight, orders[2], count, me)

    def joined(got):
        return got.reshape(count, 4, share, width).transpose(1, 0, 2, 3).reshape(
            4, width, width
        )

    parts = (joined(got_one), joined(got_two), got_three.reshape(4, width, width))
    got_small = got_small[:, 0, :small_len].astype(F32)
    vectors = jnp.concatenate(
        [
            got_small[:, : 8 * share].reshape(count, 8, share).transpose(1, 0, 2).reshape(8, width),
            got_small[:, 8 * share :].reshape(4, width),
            jnp.zeros((4, width), F32),
        ],
        axis=0,
    )

    n_win = (MAP // WIN) ** 2
    cells = (
        region_ids.reshape(MAP // WIN, WIN, MAP // WIN, WIN)
        .transpose(0, 2, 1, 3)
        .reshape(n_win, SPAN)
    )
    mask = jnp.where(cells[:, :, None] == cells[:, None, :], 0.0, MASK_FILL).astype(F32)
    mask = jnp.pad(mask, ((0, 0), (0, 0), (0, PAD - SPAN)))
    mask = jnp.pad(mask, ((0, 0), (0, PAD - SPAN), (0, 0)), constant_values=NEG)
    by_key = relative_index.T
    padded_index = jnp.pad(by_key, ((0, PAD - SPAN), (0, PAD - SPAN)), constant_values=-1)
    hot = (jnp.arange(table_rows)[:, None] == padded_index.reshape(1, -1)).astype(BF16)
    position = tn(bias_table, hot).reshape(heads, PAD, PAD)
    per_window = position[None] + mask[:, None]
    per_pair = per_window.reshape(n_win // 2, 2, heads, PAD, PAD)
    off = jnp.full((n_win // 2, heads, PAD, PAD), NEG, F32)
    bias = jnp.concatenate(
        [
            jnp.concatenate([per_pair[:, 0], off], axis=-1),
            jnp.concatenate([off, per_pair[:, 1]], axis=-1),
        ],
        axis=-2,
    ).reshape(n_win // 2, 4, 512, 128)

    act, tg, grad_a, grad_h, grad_o, gv, gs = run_block(
        counts, x_rows, c_rows, parts, vectors, bias, scale
    )

    def cut(four):
        return four.reshape(4, count, share, width).transpose(1, 0, 2, 3).reshape(
            count, 4 * share, width
        )

    small_grad = jnp.concatenate(
        [
            gv[:8].reshape(8, count, share).transpose(1, 0, 2).reshape(count, 8 * share),
            gv[8:12].reshape(count, wide),
        ],
        axis=1,
    ).astype(BF16)
    small_grad = jnp.pad(small_grad, ((0, 0), (0, width - small_len)))[:, None]
    own_one = scatter_sum(cut(grad_a), orders[0][::-1], count, me).astype(F32)
    own_two = scatter_sum(cut(grad_h), orders[1][::-1], count, me).astype(F32)
    own_small = scatter_sum(small_grad, orders[0][::-1], count, me).astype(F32)[0]
    own_three = scatter_sum(
        grad_o.reshape(count, 4 * share, width), orders[2][::-1], count, me
    ).astype(F32)

    gs = gs.reshape(heads, 128, 128)
    gs = gs[:, :SPAN, :SPAN] + gs[:, PAD : PAD + SPAN, PAD : PAD + SPAN]
    hot_back = (by_key.reshape(-1, 1) == jnp.arange(table_rows)[None, :]).astype(F32)
    table = jnp.dot(
        gs.reshape(heads, SPAN * SPAN),
        hot_back,
        precision=lax.Precision.HIGHEST,
        preferred_element_type=F32,
    )
    for bit in orders[0][::-1]:
        table = table + swap(table, bit, count)

    def piece(i):
        return own_small[i * share : (i + 1) * share]

    return (
        from_windows(act),
        from_windows(tg),
        piece(0),
        piece(1),
        jnp.concatenate([own_one[share * j : share * (j + 1)] for j in range(3)], axis=1),
        piece(2),
        piece(3),
        own_one[3 * share :],
        piece(4),
        piece(5),
        piece(6),
        jnp.concatenate([own_two[share * j : share * (j + 1)] for j in range(4)], axis=1),
        own_small[8 * share : 8 * share + wide],
        own_three,
        piece(7),
        table.T,
    )


def solution(mesh):
    row = P("dp")
    matrix = P("dp", None)
    field = P("dp", None, None, None)
    return jax.shard_map(
        functools.partial(local, count=mesh.shape["dp"]),
        mesh=mesh,
        in_specs=(
            field,
            field,
            row,
            P(),
            P(),
            row,
            row,
            matrix,
            row,
            row,
            matrix,
            row,
            row,
            row,
            matrix,
            row,
            matrix,
            row,
            P(),
        ),
        out_specs=(
            field,
            field,
            row,
            row,
            matrix,
            row,
            row,
            matrix,
            row,
            row,
            row,
            matrix,
            row,
            matrix,
            row,
            P(),
        ),
        check_vma=False,
    )
```
